1024 devices in a mesh: dp: 256 (over y_lo, z, x, core), group: 4 (over y_hi).
Axes of the slice: x: 4, y: 8 (y_hi: 4, y_lo: 2; y = y_hi * 2 + y_lo), z: 16, core: 2. Of those that a mesh axis runs over, the one named last changes fastest.
Arguments:
- image_embed: bfloat16 [131072, 1152], P(('dp', 'group')), may hold values from -6 to 6
- text_embed: bfloat16 [131072, 1152], P(('dp', 'group')), may hold values from -6 to 6
Outputs:
- grad_image: float32 [131072, 1152], P(('dp', 'group'))
- grad_text: float32 [131072, 1152], P(('dp', 'group'))
The draws below stay inside these ranges and needn't reach their ends.
All inputs are finite; a program needn't handle non-finite values.
Results may differ from the reference program's by a relative error of at most 0.0022.
Values may be sent and summed in bfloat16 or wider, within the bound.
A program may use at most 32 MiB of HBM per device.

```python
import math
import jax
import jax.numpy as jnp
from jax import lax

D = 1152
ROWS = 128
HOPS = 4
TOTAL = 131072
N_DP = 256
N_GROUP = 4


def level_of(key, extent, split, smallest, top_value):
    level, own = 1.0, jax.random.fold_in(key, 6)
    for dim, shards_of in split:
        steps = jnp.exp(jax.random.uniform(jax.random.fold_in(own, dim), (shards_of,), jnp.float32, smallest / len(split), top_value / len(split)))
        level = level * jnp.repeat(steps, extent[dim] // shards_of).reshape([-1 if axis == dim else 1 for axis in range(len(extent))])
    return level


def normal_values(key, dims, deviation, limit, split=(), kind=jnp.bfloat16):
    drawn = jax.random.normal(key, dims, jnp.float32) * deviation
    if len(split) > 0:
        drawn = level_of(key, dims, split, -0.22, 0.18) * drawn
    return jnp.clip(drawn, min=-limit, max=limit).astype(kind)


def setup_inputs(seed: int = 0) -> dict:
    key_list = jax.random.split(jax.random.key(seed), 3)
    image_embed = normal_values(key_list[0], (TOTAL, D), 1.0, 6.0, ((0, 1024),))
    text_embed = normal_values(key_list[1], (TOTAL, D), 1.0, 6.0, ((0, 1024),))
    return dict(image_embed=image_embed, text_embed=text_embed)


logit_bias = -2.0

def reference(image_embed, text_embed):
    count = N_DP * N_GROUP
    scale = 2.0 / math.sqrt(D)
    images = image_embed.reshape(count, ROWS, D).astype(jnp.float32)
    texts = text_embed.reshape(count, ROWS, D).astype(jnp.float32)
    identity = jnp.eye(ROWS, dtype=jnp.float32)
    image_sum = jnp.zeros((count, ROWS, D), jnp.float32)
    text_sum = jnp.zeros((count, ROWS, D), jnp.float32)
    for offset in range(-HOPS, HOPS + 1):
        visiting = jnp.roll(texts, -offset, axis=0)
        dots = jnp.einsum('brd,bsd->brs', images, visiting)
        coeff = jax.nn.sigmoid(scale * dots + logit_bias)
        if offset == 0:
            coeff = coeff - identity
        coeff = lax.optimization_barrier(coeff.astype(jnp.bfloat16)).astype(jnp.float32)
        image_sum = image_sum + jnp.einsum('brs,bsd->brd', coeff, visiting)
        partial_text = jnp.einsum('brs,brd->bsd', coeff, images)
        text_sum = text_sum + jnp.roll(partial_text, offset, axis=0)
    grad_image = (scale * image_sum).reshape(TOTAL, D)
    grad_text = (scale * text_sum).reshape(TOTAL, D)
    return (grad_image, grad_text)
```

```python
import math

import jax
import jax.numpy as jnp
from jax import lax
from jax.experimental import pallas as pl
from jax.experimental.pallas import tpu as pltpu
from jax.sharding import PartitionSpec as P

MESH = pl.DeviceIdType.MESH
BIAS = -2.0
ROWS = 128
CHUNKS = 4
STEP = ROWS // CHUNKS
TILE = 384

HERE, PARTNER, UP, UP_PARTNER, DOWN, DOWN_PARTNER = range(6)


def block(i):
    return pl.ds(i * ROWS, ROWS)


def part(i, k):
    return pl.ds(i * ROWS + k * STEP, STEP)


def kernel(image_ref, text_ref, grad_image_ref, grad_text_ref, images, texts, coeffs, leaving, arriving, send_sem, recv_sem, local_sem):
    h, g = lax.axis_index("dp"), lax.axis_index("group")
    n = lax.axis_size("dp")
    row_g, col_g = g ^ 1, 3 - g
    row, col = (h, row_g), (h, col_g)
    up, down = (lax.rem(h + 1, n), g), (lax.rem(h + n - 1, n), g)
    scale = 2.0 / math.sqrt(image_ref.shape[1])

    loads = [
        pltpu.make_async_copy(image_ref, images.at[block(HERE)], local_sem.at[0]),
        pltpu.make_async_copy(text_ref, texts.at[block(HERE)], local_sem.at[1]),
    ]
    for load in loads:
        load.start()

    barrier = pltpu.get_barrier_semaphore()
    for other in (row, col, up, down):
        pl.semaphore_signal(barrier, inc=1, device_id=other, device_id_type=MESH)

    image_up, image_down = g != 2, g != 1
    text_up, text_down = g >= 2, g < 2
    zero = jnp.zeros((ROWS, images.shape[1]), images.dtype)
    for needed, buf, slot in (
        (image_up, images, UP_PARTNER),
        (image_down, images, DOWN_PARTNER),
        (text_up, texts, UP_PARTNER),
        (text_down, texts, DOWN_PARTNER),
    ):

        @pl.when(jnp.logical_not(needed))
        def _(buf=buf, slot=slot):
            buf[block(slot), :] = zero

    for load in loads:
        load.wait()
    pl.semaphore_wait(barrier, 4)

    count = [0]

    def copy(src, dst, device):
        i = count[0]
        count[0] += 1
        return pltpu.make_async_remote_copy(
            src_ref=src, dst_ref=dst, send_sem=send_sem.at[i], recv_sem=recv_sem.at[i], device_id=device, device_id_type=MESH
        )

    def sent(buf, frm, to, device, k):
        return copy(buf.at[part(frm, k)], buf.at[part(to, k)], device)

    imports = [(sent(images, HERE, PARTNER, row, k), sent(texts, HERE, PARTNER, col, k)) for k in range(CHUNKS)]
    shares = [
        copy(buf.at[block(HERE)], buf.at[block(to)], device)
        for to, device in ((DOWN, up), (UP, down))
        for buf in (images, texts)
    ]
    forwards = [
        (
            (image_down, sent(images, PARTNER, DOWN_PARTNER, up, k)),
            (image_up, sent(images, PARTNER, UP_PARTNER, down, k)),
            (text_down, sent(texts, PARTNER, DOWN_PARTNER, up, k)),
            (text_up, sent(texts, PARTNER, UP_PARTNER, down, k)),
        )
        for k in range(CHUNKS)
    ]
    returns = [
        [copy(leaving.at[part(s, k)], arriving.at[part(s, k)], device) for k in range(CHUNKS)]
        for s, device in ((0, row), (1, col))
    ]

    for pair in imports:
        for c in pair:
            c.start()
    for c in shares:
        c.start()
    for k in range(CHUNKS):
        image_in, text_in = imports[k]
        fwd = forwards[k]
        image_in.wait_recv()
        for needed, c in fwd[:2]:
            pl.when(needed)(c.start)
        text_in.wait_recv()
        for needed, c in fwd[2:]:
            pl.when(needed)(c.start)

    eye = (
        lax.broadcasted_iota(jnp.int32, (ROWS, ROWS), 0) == lax.broadcasted_iota(jnp.int32, (ROWS, ROWS), 1)
    ).astype(jnp.float32)

    def fill(side, mine, others, first, last):
        my_g = (g, row_g) if side == 0 else (g, col_g)
        other_g = (g, col_g) if side == 0 else (g, row_g)
        for a in range(2):
            dots = lax.dot_general(
                mine[block(a), :],
                others[pl.ds(first * ROWS, (last - first) * ROWS), :],
                (((1,), (1,)), ((), ())),
                preferred_element_type=jnp.float32,
            )
            value = jax.nn.sigmoid(scale * dots + BIAS)
            for j in range(first, last):
                piece = value[:, (j - first) * ROWS : (j - first + 1) * ROWS]
                if j == HERE and a == 0:
                    piece = piece - eye
                if j >= UP:
                    ahead, behind = my_g[a] >= other_g[j % 2], my_g[a] <= other_g[j % 2]
                    valid = ahead if j < DOWN else behind
                    piece = piece * jnp.where(valid, 1.0, 0.0)
                coeffs[side, block(a), block(j)] = piece.astype(jnp.bfloat16)

    sides = ((0, images, texts), (1, texts, images))
    for s, mine, others in sides:
        fill(s, mine, others, HERE, UP)
    for c in shares:
        c.wait_recv()
    for k in range(CHUNKS):
        for needed, c in forwards[k]:
            pl.when(needed)(c.wait_recv)
    for s, mine, others in sides:
        fill(s, mine, others, UP, DOWN_PARTNER + 1)

    width = images.shape[1]
    for s, mine, others in sides:
        for t in range(0, width, TILE):
            leaving[block(s), t : t + TILE] = jnp.dot(
                coeffs[s, block(1), :], others[:, t : t + TILE], preferred_element_type=jnp.float32
            ).astype(jnp.bfloat16)
        for c in returns[s]:
            c.start()
    outs = (grad_image_ref, grad_text_ref)
    for s, mine, others in sides:
        for t in range(0, width, TILE):
            outs[s][:, t : t + TILE] = jnp.dot(
                coeffs[s, block(0), :], others[:, t : t + TILE], preferred_element_type=jnp.float32
            )
    for k in range(CHUNKS):
        for s in range(2):
            returns[s][k].wait_recv()
            at = pl.ds(k * STEP, STEP)
            outs[s][at, :] = scale * (outs[s][at, :] + arriving[part(s, k), :].astype(jnp.float32))

    for pair in imports:
        for c in pair:
            c.wait_send()
    for c in shares:
        c.wait_send()
    for fwd in forwards:
        for needed, c in fwd:
            pl.when(needed)(c.wait_send)
    for side in returns:
        for c in side:
            c.wait_send()


def body(image_embed, text_embed):
    rows, width = image_embed.shape
    copies = 2 * CHUNKS + 4 + 4 * CHUNKS + 2 * CHUNKS
    return pl.pallas_call(
        kernel,
        out_shape=[jax.ShapeDtypeStruct((rows, width), jnp.float32)] * 2,
        in_specs=[pl.BlockSpec(memory_space=pl.ANY)] * 2,
        out_specs=[pl.BlockSpec(memory_space=pltpu.VMEM)] * 2,
        scratch_shapes=[
            pltpu.VMEM((6 * rows, width), jnp.bfloat16),
            pltpu.VMEM((6 * rows, width), jnp.bfloat16),
            pltpu.VMEM((2, 2 * rows, 6 * rows), jnp.bfloat16),
            pltpu.VMEM((2 * rows, width), jnp.bfloat16),
            pltpu.VMEM((2 * rows, width), jnp.bfloat16),
            pltpu.SemaphoreType.DMA((copies,)),
            pltpu.SemaphoreType.DMA((copies,)),
            pltpu.SemaphoreType.DMA((2,)),
        ],
        compiler_params=pltpu.CompilerParams(
            collective_id=0, has_side_effects=True, vmem_limit_bytes=48 * 1024 * 1024
        ),
        cost_estimate=pl.CostEstimate(flops=2 * 4 * 256 * 768 * 1152, bytes_accessed=6 * rows * width * 2, transcendentals=2 * 256 * 768),
    )(image_embed, text_embed)


def solution(mesh):
    spec = P(("dp", "group"), None)
    return jax.shard_map(body, mesh=mesh, in_specs=(spec, spec), out_specs=(spec, spec), check_vma=False)
```

```python
import math

import jax
import jax.numpy as jnp
from jax import lax
from jax.experimental import pallas as pl
from jax.experimental.pallas import tpu as pltpu
from jax.sharding import PartitionSpec as P

MESH = pl.DeviceIdType.MESH
BIAS = -2.0
ROWS = 128
CHUNKS = 4
STEP = ROWS // CHUNKS
TILE = 384
VMEM_BYTES = 64 * 1024 * 1024

HERE, PARTNER, UP, UP_PARTNER, DOWN, DOWN_PARTNER = range(6)

PLANES = 2


def block(i):
    return pl.ds(pl.multiple_of(i * ROWS, ROWS), ROWS)


def part(i, k):
    return pl.ds(pl.multiple_of(i * ROWS + k * STEP, STEP), STEP)


def kernel(image_ref, text_ref, own_image_ref, own_text_ref, arriving, images, texts, coeffs, leaving, own, send_sem, recv_sem, local_sem):
    h, g = lax.axis_index("dp"), lax.axis_index("group")
    n = lax.axis_size("dp")
    plane = n // PLANES
    place = h % plane
    row_g, col_g = g ^ 1, 3 - g
    row, col = (h, row_g), (h, col_g)
    up, down = ((h + 1) % n, g), ((h + n - 1) % n, g)
    across_h = jnp.where(place == 0, h + n - 1, h + 1) % n
    across_row, across_col = (across_h, row_g), (across_h, col_g)
    first, last = place == 0, place == plane - 1
    edge = jnp.logical_or(first, last)
    scale = 2.0 / math.sqrt(image_ref.shape[1])

    loads = [
        pltpu.make_async_copy(image_ref, images.at[block(HERE)], local_sem.at[0]),
        pltpu.make_async_copy(text_ref, texts.at[block(HERE)], local_sem.at[1]),
    ]
    for load in loads:
        load.start()

    barrier = pltpu.get_barrier_semaphore()

    def greet(*others):
        for other in others:
            pl.semaphore_signal(barrier, inc=1, device_id=other, device_id_type=MESH)

    greet(row, col, up, down)
    pl.when(edge)(lambda: greet(across_row, across_col))

    image_up, image_down = g != 2, g != 1
    text_up, text_down = g >= 2, g < 2
    zero = jnp.zeros((ROWS, images.shape[1]), images.dtype)
    for needed, buf, slot in (
        (image_up, images, UP_PARTNER),
        (image_down, images, DOWN_PARTNER),
        (text_up, texts, UP_PARTNER),
        (text_down, texts, DOWN_PARTNER),
    ):

        @pl.when(jnp.logical_not(needed))
        def _(buf=buf, slot=slot):
            buf[block(slot), :] = zero

    for load in loads:
        load.wait()
    pl.semaphore_wait(barrier, jnp.where(edge, 6, 4))

    count = [0]

    def copy(src, dst, device):
        i = count[0]
        count[0] += 1
        return pltpu.make_async_remote_copy(
            src_ref=src, dst_ref=dst, send_sem=send_sem.at[i], recv_sem=recv_sem.at[i], device_id=device, device_id_type=MESH
        )

    def whole(buf, frm, to, device):
        return copy(buf.at[block(frm)], buf.at[block(to)], device)

    def piece(buf, frm, to, device, k):
        return copy(buf.at[part(frm, k)], buf.at[part(to, k)], device)

    every = range(CHUNKS)
    both = (images, texts)
    imports = [(piece(images, HERE, PARTNER, row, k), piece(texts, HERE, PARTNER, col, k)) for k in every]
    share_up = [(True, whole(buf, HERE, DOWN, up)) for buf in both]
    share_down = [(True, whole(buf, HERE, UP, down)) for buf in both]
    forward_up = [
        [(needed, piece(buf, PARTNER, DOWN_PARTNER, up, k)) for needed, buf in ((image_down, images), (text_down, texts))]
        for k in every
    ]
    forward_down = [
        [(needed, piece(buf, PARTNER, UP_PARTNER, down, k)) for needed, buf in ((image_up, images), (text_up, texts))]
        for k in every
    ]
    across = [whole(images, HERE, DOWN_PARTNER, across_row), whole(texts, HERE, DOWN_PARTNER, across_col)]
    across_out = list(zip((row_g != 1, col_g < 2), across))
    across_in = list(zip((image_down, text_down), across))
    returns = [
        [(True, copy(leaving.at[part(s, k)], arriving.at[part(s, k)], device)) for k in every] for s, device in ((0, row), (1, col))
    ]

    def each(method, *lists):
        for copies in lists:
            for needed, c in copies:
                if needed is True:
                    getattr(c, method)()
                else:
                    pl.when(needed)(getattr(c, method))

    pl.when(last)(lambda: each("start", share_up, across_out))
    for pair in imports:
        for c in pair:
            c.start()
    pl.when(jnp.logical_not(last))(lambda: each("start", share_up))
    each("start", share_down)
    for k in every:
        for i in range(2):
            imports[k][i].wait_recv()
            pl.when(jnp.logical_not(last))(lambda k=k, i=i: each("start", forward_up[k][i : i + 1]))
            each("start", forward_down[k][i : i + 1])

    eye = (
        lax.broadcasted_iota(jnp.int32, (ROWS, ROWS), 0) == lax.broadcasted_iota(jnp.int32, (ROWS, ROWS), 1)
    ).astype(jnp.float32)

    def fill(side, mine, others, begin, end):
        my_g = (g, row_g) if side == 0 else (g, col_g)
        other_g = (g, col_g) if side == 0 else (g, row_g)
        for a in range(2):
            dots = lax.dot_general(
                mine[block(a), :],
                others[begin * ROWS : end * ROWS, :],
                (((1,), (1,)), ((), ())),
                preferred_element_type=jnp.float32,
            )
            value = jax.nn.sigmoid(scale * dots + BIAS)
            for j in range(begin, end):
                some = value[:, (j - begin) * ROWS : (j - begin + 1) * ROWS]
                if j == HERE and a == 0:
                    some = some - eye
                if j >= UP:
                    ahead, behind = my_g[a] >= other_g[j % 2], my_g[a] <= other_g[j % 2]
                    valid = ahead if j < DOWN else behind
                    some = some * jnp.where(valid, 1.0, 0.0)
                coeffs[side, block(a), block(j)] = some.astype(jnp.bfloat16)

    sides = ((0, images, texts), (1, texts, images))
    for s, mine, others in sides:
        fill(s, mine, others, HERE, UP)

    each("wait_recv", share_down, *forward_down)
    for s, mine, others in sides:
        fill(s, mine, others, UP, DOWN)

    each("wait_recv", share_up)
    pl.when(first)(lambda: each("wait_recv", across_in))
    pl.when(jnp.logical_not(first))(lambda: each("wait_recv", *forward_up))

    width = images.shape[1]
    worked = (DOWN_PARTNER + 1) * ROWS
    stores = [pltpu.make_async_copy(own.at[s], ref, local_sem.at[s]) for s, ref in enumerate((own_image_ref, own_text_ref))]
    for s, mine, others in sides:
        fill(s, mine, others, DOWN, DOWN_PARTNER + 1)
        for t in range(0, width, TILE):
            leaving[block(s), t : t + TILE] = jnp.dot(
                coeffs[s, block(1), :], others[:worked, t : t + TILE], preferred_element_type=jnp.float32
            ).astype(jnp.bfloat16)
        each("start", returns[s])
    for s, mine, others in sides:
        for t in range(0, width, TILE):
            own[s, :, t : t + TILE] = jnp.dot(
                coeffs[s, block(0), :], others[:worked, t : t + TILE], preferred_element_type=jnp.float32
            )
        stores[s].start()
    for store in stores:
        store.wait()
    each("wait_recv", *returns)

    for pair in imports:
        for c in pair:
            c.wait_send()
    each("wait_send", share_up, share_down, *forward_down, *returns)
    pl.when(last)(lambda: each("wait_send", across_out))
    pl.when(jnp.logical_not(last))(lambda: each("wait_send", *forward_up))


def body(image_embed, text_embed):
    rows, width = image_embed.shape
    copies = 8 * CHUNKS + 6
    own_image, own_text, arrived = pl.pallas_call(
        kernel,
        out_shape=[jax.ShapeDtypeStruct((rows, width), jnp.float32)] * 2 + [jax.ShapeDtypeStruct((2 * rows, width), jnp.bfloat16)],
        in_specs=[pl.BlockSpec(memory_space=pl.ANY)] * 2,
        out_specs=[pl.BlockSpec(memory_space=pl.ANY)] * 3,
        scratch_shapes=[
            pltpu.VMEM((6 * rows, width), jnp.bfloat16),
            pltpu.VMEM((6 * rows, width), jnp.bfloat16),
            pltpu.VMEM((2, 2 * rows, 6 * rows), jnp.bfloat16),
            pltpu.VMEM((2 * rows, width), jnp.bfloat16),
            pltpu.VMEM((2, rows, width), jnp.float32),
            pltpu.SemaphoreType.DMA((copies,)),
            pltpu.SemaphoreType.DMA((copies,)),
            pltpu.SemaphoreType.DMA((2,)),
        ],
        compiler_params=pltpu.CompilerParams(collective_id=0, has_side_effects=True, vmem_limit_bytes=VMEM_BYTES),
    )(image_embed, text_embed)
    scale = 2.0 / math.sqrt(width)
    return (
        scale * (own_image + arrived[:rows].astype(jnp.float32)),
        scale * (own_text + arrived[rows:].astype(jnp.float32)),
    )


def solution(mesh):
    spec = P(("dp", "group"), None)
    return jax.shard_map(body, mesh=mesh, in_specs=(spec, spec), out_specs=(spec, spec), check_vma=False)
```

```python
import math

import jax
import jax.numpy as jnp
from jax import lax
from jax.experimental import pallas as pl
from jax.experimental.pallas import tpu as pltpu
from jax.sharding import PartitionSpec as P

MESH = pl.DeviceIdType.MESH
BIAS = -2.0
ROWS = 128
CHUNKS = 4
STEP = ROWS // CHUNKS
TILE = 384
VMEM_BYTES = 64 * 1024 * 1024

HERE, PARTNER, UP, UP_PARTNER, DOWN, DOWN_PARTNER = range(6)

PLANES = 2


def block(i):
    return pl.ds(pl.multiple_of(i * ROWS, ROWS), ROWS)


def part(i, k):
    return pl.ds(pl.multiple_of(i * ROWS + k * STEP, STEP), STEP)


def kernel(image_ref, text_ref, own_image_ref, own_text_ref, arriving, images, texts, coeffs, leaving, own, send_sem, recv_sem, local_sem):
    h, g = lax.axis_index("dp"), lax.axis_index("group")
    n = lax.axis_size("dp")
    plane = n // PLANES
    place = h % plane
    row_g, col_g = g ^ 1, 3 - g
    row, col = (h, row_g), (h, col_g)
    up, down = ((h + 1) % n, g), ((h + n - 1) % n, g)
    across_h = jnp.where(place == 0, h + n - 1, h + 1) % n
    across_row, across_col = (across_h, row_g), (across_h, col_g)
    first, last = place == 0, place == plane - 1
    edge = jnp.logical_or(first, last)
    scale = 2.0 / math.sqrt(image_ref.shape[1])

    loads = [
        pltpu.make_async_copy(image_ref, images.at[block(HERE)], local_sem.at[0]),
        pltpu.make_async_copy(text_ref, texts.at[block(HERE)], local_sem.at[1]),
    ]
    for load in loads:
        load.start()

    barrier = pltpu.get_barrier_semaphore()

    def greet(*others):
        for other in others:
            pl.semaphore_signal(barrier, inc=1, device_id=other, device_id_type=MESH)

    greet(row, col, up, down)
    pl.when(edge)(lambda: greet(across_row, across_col))

    image_up, image_down = g != 2, g != 1
    text_up, text_down = g >= 2, g < 2
    zero = jnp.zeros((ROWS, images.shape[1]), images.dtype)
    for needed, buf, slot in (
        (image_up, images, UP_PARTNER),
        (image_down, images, DOWN_PARTNER),
        (text_up, texts, UP_PARTNER),
        (text_down, texts, DOWN_PARTNER),
    ):

        @pl.when(jnp.logical_not(needed))
        def _(buf=buf, slot=slot):
            buf[block(slot), :] = zero

    for load in loads:
        load.wait()
    pl.semaphore_wait(barrier, jnp.where(edge, 6, 4))

    count = [0]

    def copy(src, dst, device):
        i = count[0]
        count[0] += 1
        return pltpu.make_async_remote_copy(
            src_ref=src, dst_ref=dst, send_sem=send_sem.at[i], recv_sem=recv_sem.at[i], device_id=device, device_id_type=MESH
        )

    def whole(buf, frm, to, device):
        return copy(buf.at[block(frm)], buf.at[block(to)], device)

    def piece(buf, frm, to, device, k):
        return copy(buf.at[part(frm, k)], buf.at[part(to, k)], device)

    every = range(CHUNKS)
    both = (images, texts)
    imports = [(piece(images, HERE, PARTNER, row, k), piece(texts, HERE, PARTNER, col, k)) for k in every]
    share_up = [(True, whole(buf, HERE, DOWN, up)) for buf in both]
    share_down = [(True, whole(buf, HERE, UP, down)) for buf in both]
    forward_up = [
        [(needed, piece(buf, PARTNER, DOWN_PARTNER, up, k)) for needed, buf in ((image_down, images), (text_down, texts))]
        for k in every
    ]
    forward_down = [
        [(needed, piece(buf, PARTNER, UP_PARTNER, down, k)) for needed, buf in ((image_up, images), (text_up, texts))]
        for k in every
    ]
    across = [whole(images, HERE, DOWN_PARTNER, across_row), whole(texts, HERE, DOWN_PARTNER, across_col)]
    across_out = list(zip((row_g != 1, col_g < 2), across))
    across_in = list(zip((image_down, text_down), across))
    returns = [
        [(True, copy(leaving.at[part(s, k)], arriving.at[part(s, k)], device)) for k in every] for s, device in ((0, row), (1, col))
    ]

    def each(method, *lists):
        for copies in lists:
            for needed, c in copies:
                if needed is True:
                    getattr(c, method)()
                else:
                    pl.when(needed)(getattr(c, method))

    pl.when(last)(lambda: each("start", share_up[1:], across_out[1:], across_out[:1], share_up[:1]))
    for pair in imports:
        for c in pair:
            c.start()
    pl.when(jnp.logical_not(last))(lambda: each("start", share_up))
    each("start", share_down)
    for k in every:
        for i in range(2):
            imports[k][i].wait_recv()
            pl.when(jnp.logical_not(last))(lambda k=k, i=i: each("start", forward_up[k][i : i + 1]))
            each("start", forward_down[k][i : i + 1])

    eye = (
        lax.broadcasted_iota(jnp.int32, (ROWS, ROWS), 0) == lax.broadcasted_iota(jnp.int32, (ROWS, ROWS), 1)
    ).astype(jnp.float32)

    def fill(side, mine, others, begin, end):
        my_g = (g, row_g) if side == 0 else (g, col_g)
        other_g = (g, col_g) if side == 0 else (g, row_g)
        for a in range(2):
            dots = lax.dot_general(
                mine[block(a), :],
                others[begin * ROWS : end * ROWS, :],
                (((1,), (1,)), ((), ())),
                preferred_element_type=jnp.float32,
            )
            value = jax.nn.sigmoid(scale * dots + BIAS)
            for j in range(begin, end):
                some = value[:, (j - begin) * ROWS : (j - begin + 1) * ROWS]
                if j == HERE and a == 0:
                    some = some - eye
                if j >= UP:
                    ahead, behind = my_g[a] >= other_g[j % 2], my_g[a] <= other_g[j % 2]
                    valid = ahead if j < DOWN else behind
                    some = some * jnp.where(valid, 1.0, 0.0)
                coeffs[side, block(a), block(j)] = some.astype(jnp.bfloat16)

    sides = ((0, images, texts), (1, texts, images))
    for s, mine, others in sides:
        fill(s, mine, others, HERE, UP)

    each("wait_recv", share_down, *forward_down)
    for s, mine, others in sides:
        fill(s, mine, others, UP, DOWN)

    def await_down(kind):
        this = slice(kind, kind + 1)
        each("wait_recv", share_up[this])
        pl.when(first)(lambda: each("wait_recv", across_in[this]))
        pl.when(jnp.logical_not(first))(lambda: each("wait_recv", *(pair[this] for pair in forward_up)))

    width = images.shape[1]
    worked = (DOWN_PARTNER + 1) * ROWS
    stores = [pltpu.make_async_copy(own.at[s], ref, local_sem.at[s]) for s, ref in enumerate((own_image_ref, own_text_ref))]
    for s, mine, others in sides:
        await_down(1 - s)
        fill(s, mine, others, DOWN, DOWN_PARTNER + 1)
        for t in range(0, width, TILE):
            leaving[block(s), t : t + TILE] = jnp.dot(
                coeffs[s, block(1), :], others[:worked, t : t + TILE], preferred_element_type=jnp.float32
            ).astype(jnp.bfloat16)
        each("start", returns[s])
    for s, mine, others in sides:
        for t in range(0, width, TILE):
            own[s, :, t : t + TILE] = jnp.dot(
                coeffs[s, block(0), :], others[:worked, t : t + TILE], preferred_element_type=jnp.float32
            )
        stores[s].start()
    for store in stores:
        store.wait()
    each("wait_recv", *returns)

    for pair in imports:
        for c in pair:
            c.wait_send()
    each("wait_send", share_up, share_down, *forward_down, *returns)
    pl.when(last)(lambda: each("wait_send", across_out))
    pl.when(jnp.logical_not(last))(lambda: each("wait_send", *forward_up))


def body(image_embed, text_embed):
    rows, width = image_embed.shape
    copies = 8 * CHUNKS + 6
    own_image, own_text, arrived = pl.pallas_call(
        kernel,
        out_shape=[jax.ShapeDtypeStruct((rows, width), jnp.float32)] * 2 + [jax.ShapeDtypeStruct((2 * rows, width), jnp.bfloat16)],
        in_specs=[pl.BlockSpec(memory_space=pl.ANY)] * 2,
        out_specs=[pl.BlockSpec(memory_space=pl.ANY)] * 3,
        scratch_shapes=[
            pltpu.VMEM((6 * rows, width), jnp.bfloat16),
            pltpu.VMEM((6 * rows, width), jnp.bfloat16),
            pltpu.VMEM((2, 2 * rows, 6 * rows), jnp.bfloat16),
            pltpu.VMEM((2 * rows, width), jnp.bfloat16),
            pltpu.VMEM((2, rows, width), jnp.float32),
            pltpu.SemaphoreType.DMA((copies,)),
            pltpu.SemaphoreType.DMA((copies,)),
            pltpu.SemaphoreType.DMA((2,)),
        ],
        compiler_params=pltpu.CompilerParams(collective_id=0, has_side_effects=True, vmem_limit_bytes=VMEM_BYTES),
    )(image_embed, text_embed)
    scale = 2.0 / math.sqrt(width)
    return (
        scale * (own_image + arrived[:rows].astype(jnp.float32)),
        scale * (own_text + arrived[rows:].astype(jnp.float32)),
    )


def solution(mesh):
    spec = P(("dp", "group"), None)
    return jax.shard_map(body, mesh=mesh, in_specs=(spec, spec), out_specs=(spec, spec), check_vma=False)
```

```python
import math

import jax
import jax.numpy as jnp
from jax import lax
from jax.experimental import pallas as pl
from jax.experimental.pallas import tpu as pltpu
from jax.sharding import PartitionSpec as P

MESH = pl.DeviceIdType.MESH
BIAS = -2.0
ROWS = 128
CHUNKS = 4
STEP = ROWS // CHUNKS
TILE = 384
VMEM_BYTES = 64 * 1024 * 1024

HERE, PARTNER, UP, UP_PARTNER, DOWN, DOWN_PARTNER = range(6)

PLANES = 2


def block(i):
    return pl.ds(pl.multiple_of(i * ROWS, ROWS), ROWS)


def part(i, k):
    return pl.ds(pl.multiple_of(i * ROWS + k * STEP, STEP), STEP)


def kernel(image_ref, text_ref, own_image_ref, own_text_ref, arriving, images, texts, coeffs, leaving, own, send_sem, recv_sem, local_sem):
    h, g = lax.axis_index("dp"), lax.axis_index("group")
    n = lax.axis_size("dp")
    plane = n // PLANES
    place = h % plane
    row_g, col_g = g ^ 1, 3 - g
    row, col = (h, row_g), (h, col_g)
    up, down = ((h + 1) % n, g), ((h + n - 1) % n, g)
    across_h = jnp.where(place == 0, h + n - 1, h + 1) % n
    across_row, across_col = (across_h, row_g), (across_h, col_g)
    first, last = place == 0, place == plane - 1
    edge = jnp.logical_or(first, last)
    scale = 2.0 / math.sqrt(image_ref.shape[1])

    loads = [
        pltpu.make_async_copy(image_ref, images.at[block(HERE)], local_sem.at[0]),
        pltpu.make_async_copy(text_ref, texts.at[block(HERE)], local_sem.at[1]),
    ]
    for load in loads:
        load.start()

    barrier = pltpu.get_barrier_semaphore()

    def greet(*others):
        for other in others:
            pl.semaphore_signal(barrier, inc=1, device_id=other, device_id_type=MESH)

    greet(row, col, up, down)
    pl.when(edge)(lambda: greet(across_row, across_col))

    image_up, image_down = g != 2, g != 1
    text_up, text_down = g >= 2, g < 2
    zero = jnp.zeros((ROWS, images.shape[1]), images.dtype)
    for needed, buf, slot in (
        (image_up, images, UP_PARTNER),
        (image_down, images, DOWN_PARTNER),
        (text_up, texts, UP_PARTNER),
        (text_down, texts, DOWN_PARTNER),
    ):

        @pl.when(jnp.logical_not(needed))
        def _(buf=buf, slot=slot):
            buf[block(slot), :] = zero

    for load in loads:
        load.wait()
    pl.semaphore_wait(barrier, jnp.where(edge, 6, 4))

    count = [0]

    def copy(src, dst, device):
        i = count[0]
        count[0] += 1
        return pltpu.make_async_remote_copy(
            src_ref=src, dst_ref=dst, send_sem=send_sem.at[i], recv_sem=recv_sem.at[i], device_id=device, device_id_type=MESH
        )

    def whole(buf, frm, to, device):
        return copy(buf.at[block(frm)], buf.at[block(to)], device)

    def piece(buf, frm, to, device, k):
        return copy(buf.at[part(frm, k)], buf.at[part(to, k)], device)

    every = range(CHUNKS)
    both = (images, texts)
    imports = [(piece(images, HERE, PARTNER, row, k), piece(texts, HERE, PARTNER, col, k)) for k in every]
    share_up = [(True, whole(buf, HERE, DOWN, up)) for buf in both]
    share_down = [(True, whole(buf, HERE, UP, down)) for buf in both]
    forward_up = [
        [(needed, piece(buf, PARTNER, DOWN_PARTNER, up, k)) for needed, buf in ((image_down, images), (text_down, texts))]
        for k in every
    ]
    forward_down = [
        [(needed, piece(buf, PARTNER, UP_PARTNER, down, k)) for needed, buf in ((image_up, images), (text_up, texts))]
        for k in every
    ]
    across = [whole(images, HERE, DOWN_PARTNER, across_row), whole(texts, HERE, DOWN_PARTNER, across_col)]
    across_out = list(zip((row_g != 1, col_g < 2), across))
    across_in = list(zip((image_down, text_down), across))
    returns = [
        [(True, copy(leaving.at[part(s, k)], arriving.at[part(s, k)], device)) for k in every] for s, device in ((0, row), (1, col))
    ]

    def each(method, *lists):
        for copies in lists:
            for needed, c in copies:
                if needed is True:
                    getattr(c, method)()
                else:
                    pl.when(needed)(getattr(c, method))

    pl.when(jnp.logical_and(last, g == 3))(lambda: each("start", across_out[1:], share_up[1:]))
    pl.when(jnp.logical_and(last, g != 3))(lambda: each("start", share_up[1:], across_out[1:]))
    pl.when(last)(lambda: each("start", across_out[:1], share_up[:1]))
    for pair in imports:
        for c in pair:
            c.start()
    pl.when(jnp.logical_not(last))(lambda: each("start", share_up))
    each("start", share_down)
    for k in every:
        for i in range(2):
            imports[k][i].wait_recv()
            pl.when(jnp.logical_not(last))(lambda k=k, i=i: each("start", forward_up[k][i : i + 1]))
            each("start", forward_down[k][i : i + 1])

    eye = (
        lax.broadcasted_iota(jnp.int32, (ROWS, ROWS), 0) == lax.broadcasted_iota(jnp.int32, (ROWS, ROWS), 1)
    ).astype(jnp.float32)

    def fill(side, mine, others, begin, end):
        my_g = (g, row_g) if side == 0 else (g, col_g)
        other_g = (g, col_g) if side == 0 else (g, row_g)
        for a in range(2):
            dots = lax.dot_general(
                mine[block(a), :],
                others[begin * ROWS : end * ROWS, :],
                (((1,), (1,)), ((), ())),
                preferred_element_type=jnp.float32,
            )
            value = jax.nn.sigmoid(scale * dots + BIAS)
            for j in range(begin, end):
                some = value[:, (j - begin) * ROWS : (j - begin + 1) * ROWS]
                if j == HERE and a == 0:
                    some = some - eye
                if j >= UP:
                    ahead, behind = my_g[a] >= other_g[j % 2], my_g[a] <= other_g[j % 2]
                    valid = ahead if j < DOWN else behind
                    some = some * jnp.where(valid, 1.0, 0.0)
                coeffs[side, block(a), block(j)] = some.astype(jnp.bfloat16)

    sides = ((0, images, texts), (1, texts, images))
    for s, mine, others in sides:
        fill(s, mine, others, HERE, UP)

    each("wait_recv", share_down, *forward_down)
    for s, mine, others in sides:
        fill(s, mine, others, UP, DOWN)

    def await_down(kind):
        this = slice(kind, kind + 1)
        each("wait_recv", share_up[this])
        pl.when(first)(lambda: each("wait_recv", across_in[this]))
        pl.when(jnp.logical_not(first))(lambda: each("wait_recv", *(pair[this] for pair in forward_up)))

    width = images.shape[1]
    worked = (DOWN_PARTNER + 1) * ROWS
    stores = [pltpu.make_async_copy(own.at[s], ref, local_sem.at[s]) for s, ref in enumerate((own_image_ref, own_text_ref))]
    for s, mine, others in sides:
        await_down(1 - s)
        fill(s, mine, others, DOWN, DOWN_PARTNER + 1)
        for t in range(0, width, TILE):
            leaving[block(s), t : t + TILE] = jnp.dot(
                coeffs[s, block(1), :], others[:worked, t : t + TILE], preferred_element_type=jnp.float32
            ).astype(jnp.bfloat16)
        each("start", returns[s])
    for s, mine, others in sides:
        for t in range(0, width, TILE):
            own[s, :, t : t + TILE] = jnp.dot(
                coeffs[s, block(0), :], others[:worked, t : t + TILE], preferred_element_type=jnp.float32
            )
        stores[s].start()
    for store in stores:
        store.wait()
    each("wait_recv", *returns)

    for pair in imports:
        for c in pair:
            c.wait_send()
    each("wait_send", share_up, share_down, *forward_down, *returns)
    pl.when(last)(lambda: each("wait_send", across_out))
    pl.when(jnp.logical_not(last))(lambda: each("wait_send", *forward_up))


def body(image_embed, text_embed):
    rows, width = image_embed.shape
    copies = 8 * CHUNKS + 6
    own_image, own_text, arrived = pl.pallas_call(
        kernel,
        out_shape=[jax.ShapeDtypeStruct((rows, width), jnp.float32)] * 2 + [jax.ShapeDtypeStruct((2 * rows, width), jnp.bfloat16)],
        in_specs=[pl.BlockSpec(memory_space=pl.ANY)] * 2,
        out_specs=[pl.BlockSpec(memory_space=pl.ANY)] * 3,
        scratch_shapes=[
            pltpu.VMEM((6 * rows, width), jnp.bfloat16),
            pltpu.VMEM((6 * rows, width), jnp.bfloat16),
            pltpu.VMEM((2, 2 * rows, 6 * rows), jnp.bfloat16),
            pltpu.VMEM((2 * rows, width), jnp.bfloat16),
            pltpu.VMEM((2, rows, width), jnp.float32),
            pltpu.SemaphoreType.DMA((copies,)),
            pltpu.SemaphoreType.DMA((copies,)),
            pltpu.SemaphoreType.DMA((2,)),
        ],
        compiler_params=pltpu.CompilerParams(collective_id=0, has_side_effects=True, vmem_limit_bytes=VMEM_BYTES),
    )(image_embed, text_embed)
    scale = 2.0 / math.sqrt(width)
    return (
        scale * (own_image + arrived[:rows].astype(jnp.float32)),
        scale * (own_text + arrived[rows:].astype(jnp.float32)),
    )


def solution(mesh):
    spec = P(("dp", "group"), None)
    return jax.shard_map(body, mesh=mesh, in_specs=(spec, spec), out_specs=(spec, spec), check_vma=False)
```
